512 devices in a mesh: dp: 32 (over z, core), seq: 16 (over y, x).
Axes of the slice: x: 4, y: 4, z: 16, core: 2. Of those that a mesh axis runs over, the one named last changes fastest.
Arguments:
- features: bfloat16 [262144, 1536], P(('dp', 'seq')), parts along dimension 0, may hold values from -6 to 6
- conv_taps: float32 [5, 1536], replicated, may hold values from -2.5 to 2.5
- norm_gain: float32 [1536], replicated, may hold values from 0.5 to 2
- point_weight: bfloat16 [1536, 1536], replicated, may hold values from -0.15625 to 0.15625
- donor_weight: bfloat16 [1536, 768], replicated, may hold values from -0.15625 to 0.15625
- accept_weight: bfloat16 [1536, 768], replicated, may hold values from -0.15625 to 0.15625
- donor_pos: int32 [32768], P(('dp', 'seq')), parts along dimension 0, may hold values from 0 to 8191, as said below
- accept_pos: int32 [32768], P(('dp', 'seq')), parts along dimension 0, may hold values from 0 to 8191, as said below
- pair_counts: int32 [512], P(('dp', 'seq')), parts along dimension 0, may hold values from 1 to 64, 512 in all
Outputs:
- encoded: bfloat16 [262144, 1536], P(('dp', 'seq')), parts along dimension 0
- junction: bfloat16 [32768, 768], P(('dp', 'seq')), parts along dimension 0
The draws below stay inside these ranges and needn't reach their ends.
There are 32 independent parts, one for each index of `dp`. The reference program is written for one: setup_inputs(seed, part) draws one part's arguments, and reference() takes and returns one part's arrays. A program takes and returns all parts, laid end to end along the dimension named above; an argument that names none is the same for every part. Nothing has to cross between parts.
Inputs may be any that keep to these rules, and one draw needn't show every extreme that they name: `pair_counts`: the live counts sum to 512 and the largest is exactly 64. `donor_pos`: among the 128 donor and acceptor positions of the slots s * 64 to s * 64 + 63, at most 16 lie in any one block of 512 positions r * 512 to r * 512 + 511, and exactly 16 lie in one such block. `accept_pos`: as for donor_pos, with the two lists counted together.
All inputs are finite; a program needn't handle non-finite values. No bound on the sum of `pair_counts` on one device may be relied on, other than what follows from the above.
Results may differ from the reference program's by a relative error of at most 0.0064.
Values may be sent and summed in bfloat16 or wider, within the bound.
A program may use at most 128 MiB of HBM per device.

```python
import math
import jax
import jax.numpy as jnp
import numpy as np
from jax import lax

C = 1536
H = 768
TAPS = 5
ROWS = 512
P_DEV = 64
SEQ_LEN = 8192
PAIRS = 1024
CAP = 16
N_SEQ = 16


def pair_positions(key):
    base = jax.random.fold_in(key, 7)
    key_full, key_ids, key_mix, key_off = jax.random.split(base, 4)
    count = 2 * P_DEV
    slots_all = N_SEQ * CAP
    full_owner = jax.random.randint(key_full, (N_SEQ,), 0, N_SEQ)
    id_keys = jax.random.split(key_ids, N_SEQ)
    ids = jax.vmap(lambda one: jax.random.permutation(one, slots_all))(id_keys)
    owner_ids = (ids // CAP).astype(jnp.int32)
    order_key = (owner_ids == full_owner[:, None]).astype(jnp.int32) * slots_all + jnp.arange(slots_all, dtype=jnp.int32)[None, :]
    order = jnp.argsort(order_key, axis=1)
    others = jnp.take_along_axis(owner_ids, order, axis=1)[:, :count - CAP]
    owners = jnp.concatenate([jnp.broadcast_to(full_owner[:, None], (N_SEQ, CAP)), others], axis=1)
    mix_keys = jax.random.split(key_mix, N_SEQ)
    mixing = jax.vmap(lambda one: jax.random.permutation(one, count))(mix_keys)
    owners = jnp.take_along_axis(owners, mixing, axis=1)
    offsets = jax.random.randint(key_off, (N_SEQ, count), 0, ROWS)
    positions = (owners * ROWS + offsets).astype(jnp.int32)
    return positions


def draw_donor_pos(key, part):
    return pair_positions(key)[:, :P_DEV].reshape(PAIRS)


def draw_accept_pos(key, part):
    return pair_positions(key)[:, P_DEV:].reshape(PAIRS)


def block_scale(own_key, shape, shards, least, top_value):
    loudness = 1.0
    for position, blocks in shards:
        heights = jax.random.uniform(jax.random.fold_in(jax.random.fold_in(own_key, 6), position), (blocks,), jnp.float32, least / len(shards), top_value / len(shards))
        loudness = loudness * jnp.repeat(jnp.exp(heights), shape[position] // blocks).reshape((-1,) + (1,) * (len(shape) - 1 - position))
    return loudness


def split_up(amount, total, limit, slope):
    weights = [(1 << 20) // math.isqrt(grade ** slope) + 1 for grade in range(2, amount + 1)]
    surplus, holding = total - limit - (amount - 1), [1] * (amount - 1)
    while surplus > 0:
        free = [i for i in range(amount - 1) if holding[i] < limit]
        whole, remaining = sum([weights[i] for i in free]), surplus
        for i in free:
            addition = min(limit - holding[i], max(1, remaining * weights[i] // whole), surplus)
            holding[i] = holding[i] + addition
            surplus = surplus - addition
    return np.array([limit] + holding)


def ragged_sizes(key, amount, total, reach, lean):
    if amount == 2:
        one = jax.random.randint(key, (), max(1, total - reach), min(reach, total - 1) + 1)
        return jnp.stack([one, total - one])
    tallies = jnp.asarray(split_up(amount, total, reach, lean), jnp.int32)
    pairs = (amount - 1) // 2
    source_of, sink = tallies[1:1 + 2 * pairs:2], tallies[2:2 + 2 * pairs:2]
    margin = jnp.minimum(source_of - 1, reach - sink)
    passed = jax.random.randint(jax.random.fold_in(key, 1), (pairs,), 0, 1 << 20) % (margin + 1)
    tallies = tallies.at[1:1 + 2 * pairs:2].set(source_of - passed).at[2:2 + 2 * pairs:2].set(sink + passed)
    return tallies[jax.random.permutation(jax.random.fold_in(key, 2), amount)]


def noise(stream_key, dims, deviation, most, shards=(), kind=jnp.bfloat16):
    loudness = block_scale(stream_key, dims, shards, -0.22, 0.18) if shards else 1.0
    entries = jax.random.normal(stream_key, dims, jnp.float32) * deviation * loudness
    return jnp.minimum(jnp.maximum(entries, -most), most).astype(kind)


def setup_inputs(seed: int = 0, part: int = 0) -> dict:
    arg_keys = jax.random.split(jax.random.key(seed), 10)
    part_splits = jax.random.split(jax.random.fold_in(arg_keys[9], part), 10)
    return {
        "features": noise(part_splits[0], (SEQ_LEN, C), 1.0, 6.0, ((0, 16),)),
        "conv_taps": noise(arg_keys[1], (TAPS, C), TAPS ** -0.5, 2.5, (), jnp.float32),
        "norm_gain": jnp.clip(jnp.exp(jax.random.uniform(arg_keys[2], (C,), jnp.float32, math.log(0.5), math.log(2.0))), 0.5, 2.0),
        "point_weight": noise(arg_keys[3], (C, C), C ** -0.5, 0.15625),
        "donor_weight": noise(arg_keys[4], (C, H), C ** -0.5, 0.15625),
        "accept_weight": noise(arg_keys[5], (C, H), C ** -0.5, 0.15625),
        "donor_pos": draw_donor_pos(jax.random.fold_in(jax.random.fold_in(arg_keys[9], part), 71), part),
        "accept_pos": draw_accept_pos(jax.random.fold_in(jax.random.fold_in(arg_keys[9], part), 71), part),
        "pair_counts": ragged_sizes(part_splits[8], N_SEQ, N_SEQ * P_DEV // 2, P_DEV, 2).astype(jnp.int32),
    }


def reference(features, conv_taps, norm_gain, point_weight, donor_weight, accept_weight, donor_pos, accept_pos, pair_counts):
    padded = jnp.pad(features.astype(jnp.float32), ((2, 2), (0, 0)))
    conv = jnp.zeros((SEQ_LEN, C), jnp.float32)
    for k in range(TAPS):
        conv = conv + conv_taps[k][None, :] * padded[k:k + SEQ_LEN]
    scale = jax.lax.rsqrt(lax.optimization_barrier(jnp.mean(conv * conv, axis=-1, keepdims=True)) + 1e-06)
    normed = (conv * scale * norm_gain[None, :]).astype(jnp.bfloat16)
    mixed = jnp.dot(normed, point_weight, preferred_element_type=jnp.float32)
    encoded = (features.astype(jnp.float32) + jax.nn.gelu(mixed, approximate=False)).astype(jnp.bfloat16)
    donor_rows = jnp.take(encoded, donor_pos.astype(jnp.int32), axis=0)
    accept_rows = jnp.take(encoded, accept_pos.astype(jnp.int32), axis=0)
    slots = jnp.arange(P_DEV, dtype=jnp.int32)[None, :]
    live = (slots < pair_counts.astype(jnp.int32)[:, None]).reshape(PAIRS)
    left = jnp.dot(donor_rows, donor_weight, preferred_element_type=jnp.float32)
    right = jnp.dot(accept_rows, accept_weight, preferred_element_type=jnp.float32)
    junction = jnp.where(live[:, None], jax.nn.silu(left) * right, jnp.float32(0.0)).astype(jnp.bfloat16)
    return (encoded, junction)
```

```python
import functools

import jax
import jax.numpy as jnp
from jax import lax
from jax.experimental import pallas as pl
from jax.experimental.pallas import tpu as pltpu
from jax.sharding import PartitionSpec as P

CAP = 16
LANES = 128
WIDE = 256


def gelu(v):
    return 0.5 * v * (1.0 + lax.erf(v * 0.7071067811865476))


def kernel(
    side,
    feat_hbm,
    taps_hbm,
    gain_hbm,
    point_hbm,
    donor_hbm,
    accept_hbm,
    dpos_hbm,
    apos_hbm,
    count_hbm,
    enc_hbm,
    junc_hbm,
    feat,
    taps,
    gain,
    point,
    donor,
    accept,
    dpos,
    apos,
    count,
    padded,
    normed,
    enc,
    junc,
    hot,
    kinds,
    picked,
    edge_out,
    edge_in,
    asks,
    out_rows,
    in_rows,
    load_sem,
    store_sem,
    edge_send,
    edge_recv,
    ask_send,
    ask_recv,
    row_send,
    row_recv,
):
    n = side * side
    rows, channels = feat.shape
    slots = dpos.shape[1]
    width = donor.shape[1]
    lanes = channels // LANES
    me = lax.axis_index("seq")
    my, mx = lax.div(me, side), lax.rem(me, side)

    def ahead(d):
        y = lax.rem(my + lax.div(d, side), side)
        x = lax.rem(mx + lax.rem(d, side), side)
        return y * side + x

    def load(i, source, target):
        return pltpu.make_async_copy(source, target, load_sem.at[i])

    loads = [
        load(0, dpos_hbm, dpos),
        load(1, apos_hbm, apos),
        load(2, count_hbm, count),
        load(3, feat_hbm, feat),
        load(4, taps_hbm, taps),
        load(5, gain_hbm, gain),
        load(6, point_hbm, point),
        load(7, donor_hbm, donor),
        load(8, accept_hbm, accept),
    ]
    for one in loads:
        one.start()

    barrier = pltpu.get_barrier_semaphore()

    @pl.loop(1, n)
    def _(d):
        pl.semaphore_signal(barrier, inc=1, device_id={"seq": ahead(d)})

    loads[0].wait()
    loads[1].wait()
    sub = lax.broadcasted_iota(jnp.int32, (slots, slots), 0)
    lane = lax.broadcasted_iota(jnp.int32, (slots, slots), 1)

    def as_column(row):
        return jnp.sum(
            jnp.where(sub == lane, row.astype(jnp.float32), 0.0), axis=1, keepdims=True
        ).astype(jnp.int32)

    drow, arow = dpos[...], apos[...]
    dcol, acol = as_column(drow), as_column(arow)

    def same(col, row):
        return (col >> 9) == (row >> 9)

    def ones(mask, axis):
        return jnp.sum(jnp.where(mask, 1.0, 0.0), axis=axis, keepdims=True).astype(jnp.int32)

    drank_row = ones(same(dcol, drow) & (sub < lane), 0)
    arank_row = ones(same(acol, arow) & (sub < lane), 0) + ones(same(dcol, arow), 0)
    drank_col = ones(same(dcol, drow) & (lane < sub), 1)
    arank_col = ones(same(acol, arow) & (lane < sub), 1) + ones(same(acol, drow), 1)
    dcode = (dcol >> 9) * CAP + drank_col
    acode = (acol >> 9) * CAP + arank_col
    asks[me, 0:1, :] = (((drow >> 9) * CAP + drank_row) << 9) + (drow & (rows - 1))
    asks[me, 1:2, :] = (((arow >> 9) * CAP + arank_row) << 9) + (arow & (rows - 1))

    loads[3].wait()
    edge_out[0] = feat[0:16, :].astype(jnp.float32)[0:2]
    edge_out[1] = feat[rows - 16 : rows, :].astype(jnp.float32)[14:16]

    pl.semaphore_wait(barrier, n - 1)

    def edge(i, step):
        return pltpu.make_async_remote_copy(
            edge_out.at[i],
            edge_in.at[i],
            edge_send.at[i],
            edge_recv.at[i],
            device_id={"seq": lax.rem(me + step, n)},
        )

    before, after = edge(1, 1), edge(0, n - 1)
    before.start()
    after.start()

    def ask(d):
        return pltpu.make_async_remote_copy(
            asks.at[me], asks.at[me], ask_send.at[d], ask_recv.at[d], device_id={"seq": ahead(d)}
        )

    @pl.loop(1, n)
    def _(d):
        ask(d).start()

    loads[4].wait()
    loads[5].wait()

    @pl.loop(0, rows // 16, unroll=4)
    def _(i):
        at = pl.multiple_of(i * 16, 16)
        padded[pl.ds(at + 8, 16), :] = feat[pl.ds(at, 16), :].astype(jnp.float32)

    def conv_norm(at):
        at = pl.multiple_of(at, 16)
        total = jnp.zeros((16, LANES), jnp.float32)
        parts = []
        for c in range(lanes):
            cols = pl.ds(c * LANES, LANES)
            block = padded[pl.ds(at, 32), cols]
            conv = taps[0:1, cols] * block[6:22]
            for k in range(1, 5):
                conv = conv + taps[k : k + 1, cols] * block[6 + k : 22 + k]
            total = total + conv * conv
            parts.append(conv)
        mean = jnp.sum(total, axis=1, keepdims=True) * (1.0 / channels)
        scale = lax.rsqrt(mean + 1e-6)
        for c in range(lanes):
            cols = pl.ds(c * LANES, LANES)
            normed[pl.ds(at, 16), cols] = (parts[c] * scale * gain[c : c + 1, :]).astype(jnp.bfloat16)

    @pl.loop(1, rows // 16 - 1, unroll=2)
    def _(i):
        conv_norm(i * 16)

    before.wait()
    after.wait()
    zero = jnp.zeros((6, channels), jnp.float32)
    head = jnp.where(me == 0, 0.0, edge_in[1])
    tail = jnp.where(me == n - 1, 0.0, edge_in[0])
    padded[0:8, :] = jnp.concatenate([zero, head], axis=0)
    padded[rows + 8 : rows + 16, :] = jnp.concatenate([tail, zero], axis=0)
    conv_norm(0)
    conv_norm(rows - 16)

    @pl.loop(1, n)
    def _(d):
        ask(d).wait()

    target = me * CAP + lax.broadcasted_iota(jnp.int32, (CAP, slots), 0)
    place = lax.broadcasted_iota(jnp.int32, (CAP, rows), 1)
    for s in range(n):
        d, a = asks[s, 0:1, :], asks[s, 1:2, :]
        found = jnp.where((d >> 9) == target, (d & (rows - 1)).astype(jnp.float32), 0.0)
        found += jnp.where((a >> 9) == target, ((a & (rows - 1)) + rows).astype(jnp.float32), 0.0)
        index = jnp.sum(found, axis=1, keepdims=True).astype(jnp.int32)
        hot[s * CAP : (s + 1) * CAP, :] = jnp.where(
            (index & (rows - 1)) == place, 1.0, 0.0
        ).astype(jnp.bfloat16)
        kinds[s * CAP : (s + 1) * CAP, :] = jnp.broadcast_to(index, (CAP, LANES))

    loads[6].wait()
    stores = []
    for c in range(channels // WIDE):
        cols = slice(c * WIDE, (c + 1) * WIDE)
        mixed = jnp.dot(normed[...], point[:, cols], preferred_element_type=jnp.float32)
        enc[:, cols] = (feat[:, cols].astype(jnp.float32) + gelu(mixed)).astype(jnp.bfloat16)
        picked[:, cols] = jnp.dot(
            hot[...], enc[:, cols], preferred_element_type=jnp.float32
        ).astype(jnp.bfloat16)
    store = pltpu.make_async_copy(enc, enc_hbm, store_sem.at[0])
    store.start()

    loads[7].wait()
    loads[8].wait()
    is_accept = jnp.concatenate([kinds[...] >= rows] * (WIDE // LANES), axis=1)
    for c in range(width // WIDE):
        cols = slice(c * WIDE, (c + 1) * WIDE)
        left = jnp.dot(picked[...], donor[:, cols], preferred_element_type=jnp.float32)
        right = jnp.dot(picked[...], accept[:, cols], preferred_element_type=jnp.float32)
        out_rows[:, :, cols] = (
            jnp.where(is_accept, right, left).astype(jnp.bfloat16).reshape(n, CAP, WIDE)
        )

    def send(d):
        return pltpu.make_async_remote_copy(
            out_rows.at[ahead(d)],
            in_rows.at[me],
            row_send.at[d],
            row_recv.at[d],
            device_id={"seq": ahead(d)},
        )

    @pl.loop(1, n)
    def _(d):
        send(d).start()

    in_rows[me] = out_rows[me]
    loads[2].wait()
    live = lax.broadcasted_iota(jnp.int32, (slots, width), 0) < count[0]
    spot = lax.broadcasted_iota(jnp.int32, (slots, n * CAP), 1)
    dhot = jnp.where(spot == dcode, 1.0, 0.0).astype(jnp.bfloat16)
    ahot = jnp.where(spot == acode, 1.0, 0.0).astype(jnp.bfloat16)

    @pl.loop(1, n)
    def _(d):
        send(d).wait()

    got = in_rows[...].reshape(n * CAP, width)
    left = jnp.dot(dhot, got, preferred_element_type=jnp.float32)
    right = jnp.dot(ahot, got, preferred_element_type=jnp.float32)
    gated = left / (1.0 + jnp.exp(-left)) * right
    junc[...] = jnp.where(live, gated, 0.0).astype(jnp.bfloat16)
    last = pltpu.make_async_copy(junc, junc_hbm, store_sem.at[1])
    last.start()
    last.wait()
    store.wait()


def on_device(side, features, taps, gain, point, donor, accept, dpos, apos, counts):
    rows, channels = features.shape
    slots = dpos.shape[0]
    width = donor.shape[1]
    n = side * side
    f32, bf16, i32 = jnp.float32, jnp.bfloat16, jnp.int32
    dma = pltpu.SemaphoreType.DMA
    return pl.pallas_call(
        functools.partial(kernel, side),
        out_shape=(
            jax.ShapeDtypeStruct((rows, channels), bf16),
            jax.ShapeDtypeStruct((slots, width), bf16),
        ),
        in_specs=[pl.BlockSpec(memory_space=pltpu.HBM)] * 9,
        out_specs=[pl.BlockSpec(memory_space=pl.ANY)] * 2,
        scratch_shapes=[
            pltpu.VMEM((rows, channels), bf16),
            pltpu.VMEM(taps.shape, f32),
            pltpu.VMEM((channels // LANES, LANES), f32),
            pltpu.VMEM((channels, channels), bf16),
            pltpu.VMEM((channels, width), bf16),
            pltpu.VMEM((channels, width), bf16),
            pltpu.VMEM((1, slots), i32),
            pltpu.VMEM((1, slots), i32),
            pltpu.SMEM((1,), i32),
            pltpu.VMEM((rows + 16, channels), f32),
            pltpu.VMEM((rows, channels), bf16),
            pltpu.VMEM((rows, channels), bf16),
            pltpu.VMEM((slots, width), bf16),
            pltpu.VMEM((n * CAP, rows), bf16),
            pltpu.VMEM((n * CAP, LANES), i32),
            pltpu.VMEM((n * CAP, channels), bf16),
            pltpu.VMEM((2, 2, channels), f32),
            pltpu.VMEM((2, 2, channels), f32),
            pltpu.VMEM((n, 2, slots), i32),
            pltpu.VMEM((n, CAP, width), bf16),
            pltpu.VMEM((n, CAP, width), bf16),
            dma((9,)),
            dma((2,)),
            dma((2,)),
            dma((2,)),
            dma((n,)),
            dma((n,)),
            dma((n,)),
            dma((n,)),
        ],
        compiler_params=pltpu.CompilerParams(
            collective_id=0, has_side_effects=True, vmem_limit_bytes=56 * 1024 * 1024
        ),
        cost_estimate=pl.CostEstimate(
            flops=2 * rows * channels * channels,
            bytes_accessed=12 * 1024 * 1024,
            transcendentals=rows * channels,
        ),
    )(
        features,
        taps,
        gain.reshape(channels // LANES, LANES),
        point,
        donor,
        accept,
        dpos.reshape(1, slots),
        apos.reshape(1, slots),
        counts,
    )


def solution(mesh):
    side = 4
    placed = (
        P(("dp", "seq"), None),
        P(),
        P(),
        P(),
        P(),
        P(),
        P(("dp", "seq")),
        P(("dp", "seq")),
        P(("dp", "seq")),
    )
    return jax.shard_map(
        functools.partial(on_device, side),
        mesh=mesh,
        in_specs=placed,
        out_specs=(P(("dp", "seq"), None), P(("dp", "seq"), None)),
        check_vma=False,
    )
```

```python
import functools

import jax
import jax.numpy as jnp
from jax import lax
from jax.experimental import pallas as pl
from jax.experimental.pallas import tpu as pltpu
from jax.sharding import PartitionSpec as P

CAP = 16
LANES = 128
WIDE = 256


def gelu(v):
    return 0.5 * v * (1.0 + lax.erf(v * 0.7071067811865476))


def kernel(
    side,
    feat_hbm,
    taps_hbm,
    gain_hbm,
    point_hbm,
    donor_hbm,
    accept_hbm,
    dpos_hbm,
    apos_hbm,
    count,
    enc,
    in_rows,
    dhot,
    ahot,
    feat,
    taps,
    gain,
    point,
    donor,
    accept,
    dpos,
    apos,
    padded,
    normed,
    hot,
    kinds,
    picked,
    edge_out,
    edge_in,
    asks,
    out_rows,
    load_sem,
    edge_send,
    edge_recv,
    ask_send,
    ask_recv,
    row_send,
    row_recv,
):
    n = side * side
    rows, channels = feat.shape
    slots = dpos.shape[1]
    width = donor.shape[1]
    lanes = channels // LANES
    me = lax.axis_index("seq")
    my, mx = lax.div(me, side), lax.rem(me, side)

    def ahead(d):
        y = lax.rem(my + lax.div(d, side), side)
        x = lax.rem(mx + lax.rem(d, side), side)
        return y * side + x

    def load(i, source, target):
        return pltpu.make_async_copy(source, target, load_sem.at[i])

    loads = [
        load(0, dpos_hbm, dpos),
        load(1, apos_hbm, apos),
        load(2, feat_hbm, feat),
        load(3, taps_hbm, taps),
        load(4, gain_hbm, gain),
        load(5, point_hbm, point),
        load(6, donor_hbm, donor),
        load(7, accept_hbm, accept),
    ]
    for one in loads:
        one.start()

    barrier = pltpu.get_barrier_semaphore()

    @pl.loop(1, n)
    def _(d):
        pl.semaphore_signal(barrier, inc=1, device_id={"seq": ahead(d)})

    loads[0].wait()
    loads[1].wait()
    sub = lax.broadcasted_iota(jnp.int32, (slots, slots), 0)
    lane = lax.broadcasted_iota(jnp.int32, (slots, slots), 1)

    def as_column(row):
        return jnp.sum(
            jnp.where(sub == lane, row.astype(jnp.float32), 0.0), axis=1, keepdims=True
        ).astype(jnp.int32)

    drow, arow = dpos[...], apos[...]
    dcol, acol = as_column(drow), as_column(arow)

    def same(col, row):
        return (col >> 9) == (row >> 9)

    def ones(mask, axis):
        return jnp.sum(jnp.where(mask, 1.0, 0.0), axis=axis, keepdims=True).astype(jnp.int32)

    drank_row = ones(same(dcol, drow) & (sub < lane), 0)
    arank_row = ones(same(acol, arow) & (sub < lane), 0) + ones(same(dcol, arow), 0)
    drank_col = ones(same(dcol, drow) & (lane < sub), 1)
    arank_col = ones(same(acol, arow) & (lane < sub), 1) + ones(same(acol, drow), 1)
    dcode = (dcol >> 9) * CAP + drank_col
    acode = (acol >> 9) * CAP + arank_col
    asks[me, 0:1, :] = (((drow >> 9) * CAP + drank_row) << 9) + (drow & (rows - 1))
    asks[me, 1:2, :] = (((arow >> 9) * CAP + arank_row) << 9) + (arow & (rows - 1))
    spot = lax.broadcasted_iota(jnp.int32, (slots, n * CAP), 1)
    slot = lax.broadcasted_iota(jnp.int32, (slots, n * CAP), 0)
    live = slot < count[0]
    dhot[...] = jnp.where((spot == dcode) & live, 1.0, 0.0).astype(jnp.bfloat16)
    ahot[...] = jnp.where(spot == acode, 1.0, 0.0).astype(jnp.bfloat16)

    loads[2].wait()
    loads[3].wait()
    loads[4].wait()

    def widen(at, count):
        for c in range(lanes):
            padded[c, at + 8 : at + 8 + count, :] = feat[
                at : at + count, c * LANES : (c + 1) * LANES
            ].astype(jnp.float32)

    def conv_norm(at, count):
        total = jnp.zeros((count, LANES), jnp.float32)
        parts = []
        for c in range(lanes):
            cols = slice(c * LANES, (c + 1) * LANES)
            conv = taps[0:1, cols] * padded[c, at + 6 : at + 6 + count, :]
            for k in range(1, 5):
                conv = conv + taps[k : k + 1, cols] * padded[c, at + 6 + k : at + 6 + k + count, :]
            total = total + conv * conv
            parts.append(conv)
        mean = jnp.sum(total, axis=1, keepdims=True) * (1.0 / channels)
        scale = lax.rsqrt(mean + 1e-6)
        for c in range(lanes):
            cols = slice(c * LANES, (c + 1) * LANES)
            normed[at : at + count, cols] = (parts[c] * scale * gain[c : c + 1, :]).astype(
                jnp.bfloat16
            )

    widen(0, 32)
    for at in range(16, rows - 16, 32):
        widen(at + 16, min(32, rows - at - 16))
        conv_norm(at, min(32, rows - 16 - at))
    for c in range(lanes):
        edge_out[0, 2 * c : 2 * c + 2, :] = padded[c, 8:10, :]
        edge_out[1, 2 * c : 2 * c + 2, :] = padded[c, rows + 6 : rows + 8, :]

    pl.semaphore_wait(barrier, n - 1)

    def edge(i, step):
        return pltpu.make_async_remote_copy(
            edge_out.at[i],
            edge_in.at[i],
            edge_send.at[i],
            edge_recv.at[i],
            device_id={"seq": lax.rem(me + step, n)},
        )

    def ask(d):
        return pltpu.make_async_remote_copy(
            asks.at[me], asks.at[me], ask_send.at[d], ask_recv.at[d], device_id={"seq": ahead(d)}
        )

    before, after = edge(1, 1), edge(0, n - 1)
    before.start()
    after.start()

    @pl.loop(1, n)
    def _(d):
        ask(d).start()

    loads[5].wait()

    def encode(spans):
        for c in range(channels // WIDE):
            cols = slice(c * WIDE, (c + 1) * WIDE)
            source = jnp.concatenate([normed[a:b, :] for a, b in spans], axis=0)
            mixed = jnp.dot(source, point[:, cols], preferred_element_type=jnp.float32)
            at = 0
            for a, b in spans:
                part = mixed[at : at + b - a]
                at += b - a
                enc[a:b, cols] = (feat[a:b, cols].astype(jnp.float32) + gelu(part)).astype(
                    jnp.bfloat16
                )

    encode([(16, rows - 16)])
    loads[6].wait()
    loads[7].wait()
    before.wait()
    after.wait()

    @pl.loop(1, n)
    def _(d):
        ask(d).wait()

    for c in range(lanes):
        padded[c, 6:8, :] = jnp.where(me == 0, 0.0, edge_in[1, 2 * c : 2 * c + 2, :])
        padded[c, rows + 8 : rows + 10, :] = jnp.where(
            me == n - 1, 0.0, edge_in[0, 2 * c : 2 * c + 2, :]
        )
    conv_norm(0, 16)
    conv_norm(rows - 16, 16)
    encode([(0, 16), (rows - 16, rows)])

    target = me * CAP + lax.broadcasted_iota(jnp.int32, (CAP, slots), 0)
    place = lax.broadcasted_iota(jnp.int32, (CAP, rows), 1)
    for s in range(n):
        d, a = asks[s, 0:1, :], asks[s, 1:2, :]
        found = jnp.where((d >> 9) == target, (d & (rows - 1)).astype(jnp.float32), 0.0)
        found += jnp.where((a >> 9) == target, ((a & (rows - 1)) + rows).astype(jnp.float32), 0.0)
        index = jnp.sum(found, axis=1, keepdims=True).astype(jnp.int32)
        hot[s * CAP : (s + 1) * CAP, :] = jnp.where(
            (index & (rows - 1)) == place, 1.0, 0.0
        ).astype(jnp.bfloat16)
        kinds[s * CAP : (s + 1) * CAP, :] = jnp.broadcast_to(index, (CAP, LANES))

    for c in range(channels // WIDE):
        cols = slice(c * WIDE, (c + 1) * WIDE)
        picked[:, cols] = jnp.dot(
            hot[...], enc[:, cols], preferred_element_type=jnp.float32
        ).astype(jnp.bfloat16)

    def send(c, d):
        return pltpu.make_async_remote_copy(
            out_rows.at[c, ahead(d)],
            in_rows.at[c, me],
            row_send.at[c, d],
            row_recv.at[c, d],
            device_id={"seq": ahead(d)},
        )

    is_accept = jnp.concatenate([kinds[...] >= rows] * (WIDE // LANES), axis=1)
    for c in range(width // WIDE):
        cols = slice(c * WIDE, (c + 1) * WIDE)
        left = jnp.dot(picked[...], donor[:, cols], preferred_element_type=jnp.float32)
        right = jnp.dot(picked[...], accept[:, cols], preferred_element_type=jnp.float32)
        out_rows[c] = jnp.where(is_accept, right, left).astype(jnp.bfloat16).reshape(n, CAP, WIDE)

        @pl.loop(1, n)
        def _(d):
            send(c, d).start()

    for c in range(width // WIDE):
        in_rows[c, me] = out_rows[c, me]

        @pl.loop(1, n)
        def _(d):
            send(c, d).wait()


def finish(enc, in_rows, dhot, ahot, enc_hbm, junc_hbm, junc, sem):
    store = pltpu.make_async_copy(enc, enc_hbm, sem.at[0])
    store.start()
    blocks, n, cap, wide = in_rows.shape
    for c in range(blocks):
        got = in_rows[c].reshape(n * cap, wide)
        left = jnp.dot(dhot[...], got, preferred_element_type=jnp.float32)
        right = jnp.dot(ahot[...], got, preferred_element_type=jnp.float32)
        junc[:, c * wide : (c + 1) * wide] = (left / (1.0 + jnp.exp(-left)) * right).astype(
            jnp.bfloat16
        )
    last = pltpu.make_async_copy(junc, junc_hbm, sem.at[1])
    last.start()
    last.wait()
    store.wait()


def on_device(side, features, taps, gain, point, donor, accept, dpos, apos, counts):
    rows, channels = features.shape
    slots = dpos.shape[0]
    width = donor.shape[1]
    n = side * side
    blocks = width // WIDE
    f32, bf16, i32 = jnp.float32, jnp.bfloat16, jnp.int32
    dma = pltpu.SemaphoreType.DMA
    held = pl.pallas_call(
        functools.partial(kernel, side),
        out_shape=(
            pltpu.VMEM((rows, channels), bf16),
            pltpu.VMEM((blocks, n, CAP, WIDE), bf16),
            pltpu.VMEM((slots, n * CAP), bf16),
            pltpu.VMEM((slots, n * CAP), bf16),
        ),
        in_specs=[pl.BlockSpec(memory_space=pltpu.HBM)] * 8
        + [pl.BlockSpec(memory_space=pltpu.SMEM)],
        out_specs=[pl.BlockSpec(memory_space=pltpu.VMEM)] * 4,
        scratch_shapes=[
            pltpu.VMEM((rows, channels), bf16),
            pltpu.VMEM(taps.shape, f32),
            pltpu.VMEM((channels // LANES, LANES), f32),
            pltpu.VMEM((channels, channels), bf16),
            pltpu.VMEM((channels, width), bf16),
            pltpu.VMEM((channels, width), bf16),
            pltpu.VMEM((1, slots), i32),
            pltpu.VMEM((1, slots), i32),
            pltpu.VMEM((channels // LANES, rows + 16, LANES), f32),
            pltpu.VMEM((rows, channels), bf16),
            pltpu.VMEM((n * CAP, rows), bf16),
            pltpu.VMEM((n * CAP, LANES), i32),
            pltpu.VMEM((n * CAP, channels), bf16),
            pltpu.VMEM((2, 2 * channels // LANES, LANES), f32),
            pltpu.VMEM((2, 2 * channels // LANES, LANES), f32),
            pltpu.VMEM((n, 2, slots), i32),
            pltpu.VMEM((blocks, n, CAP, WIDE), bf16),
            dma((8,)),
            dma((2,)),
            dma((2,)),
            dma((n,)),
            dma((n,)),
            dma((blocks, n)),
            dma((blocks, n)),
        ],
        compiler_params=pltpu.CompilerParams(
            collective_id=0, has_side_effects=True, vmem_limit_bytes=40 * 1024 * 1024
        ),
    )(
        *(
            pltpu.with_memory_space_constraint(v, pltpu.HBM)
            for v in (
                features,
                taps,
                gain.reshape(channels // LANES, LANES),
                point,
                donor,
                accept,
                dpos.reshape(1, slots),
                apos.reshape(1, slots),
            )
        ),
        counts,
    )
    return pl.pallas_call(
        finish,
        out_shape=(
            jax.ShapeDtypeStruct((rows, channels), bf16),
            jax.ShapeDtypeStruct((slots, width), bf16),
        ),
        in_specs=[pl.BlockSpec(memory_space=pltpu.VMEM)] * 4,
        out_specs=[pl.BlockSpec(memory_space=pltpu.HBM)] * 2,
        scratch_shapes=[pltpu.VMEM((slots, width), bf16), dma((2,))],
        compiler_params=pltpu.CompilerParams(vmem_limit_bytes=8 * 1024 * 1024),
    )(*held)


def solution(mesh):
    side = 4
    placed = (
        P(("dp", "seq"), None),
        P(),
        P(),
        P(),
        P(),
        P(),
        P(("dp", "seq")),
        P(("dp", "seq")),
        P(("dp", "seq")),
    )
    return jax.shard_map(
        functools.partial(on_device, side),
        mesh=mesh,
        in_specs=placed,
        out_specs=(P(("dp", "seq"), None), P(("dp", "seq"), None)),
        check_vma=False,
    )
```

```python
import functools

import jax
import jax.numpy as jnp
from jax import lax
from jax.experimental import pallas as pl
from jax.experimental.pallas import tpu as pltpu
from jax.sharding import PartitionSpec as P

CAP = 16
LANES = 128
WIDE = 256


def gelu(v):
    return 0.5 * v * (1.0 + lax.erf(v * 0.7071067811865476))


def kernel(
    side,
    feat_hbm,
    taps_hbm,
    gain_hbm,
    point_hbm,
    donor_hbm,
    accept_hbm,
    dpos_hbm,
    apos_hbm,
    count,
    enc,
    in_rows,
    dhot,
    ahot,
    feat,
    taps,
    gain,
    point,
    donor,
    accept,
    dpos,
    apos,
    padded,
    normed,
    hot,
    kinds,
    picked,
    edge_out,
    edge_in,
    asks,
    out_rows,
    load_sem,
    edge_send,
    edge_recv,
    ask_send,
    ask_recv,
    row_send,
    row_recv,
):
    n = side * side
    rows, channels = feat.shape
    slots = dpos.shape[1]
    width = donor.shape[1]
    lanes = channels // LANES
    me = lax.axis_index("seq")
    my, mx = lax.div(me, side), lax.rem(me, side)

    def ahead(d):
        y = lax.rem(my + lax.div(d, side), side)
        x = lax.rem(mx + lax.rem(d, side), side)
        return y * side + x

    def load(i, source, target):
        return pltpu.make_async_copy(source, target, load_sem.at[i])

    loads = [
        load(0, dpos_hbm, dpos),
        load(1, apos_hbm, apos),
        load(2, feat_hbm.at[0:16], feat.at[0:16]),
        load(3, feat_hbm.at[rows - 16 : rows], feat.at[rows - 16 : rows]),
        load(4, taps_hbm, taps),
        load(5, gain_hbm, gain),
        load(6, feat_hbm.at[16 : rows - 16], feat.at[16 : rows - 16]),
        load(7, point_hbm, point),
        load(8, donor_hbm, donor),
        load(9, accept_hbm, accept),
    ]
    barrier = pltpu.get_barrier_semaphore()

    @pl.loop(1, n)
    def _(d):
        pl.semaphore_signal(barrier, inc=1, device_id={"seq": ahead(d)})

    for one in loads:
        one.start()

    loads[0].wait()
    loads[1].wait()
    sub = lax.broadcasted_iota(jnp.int32, (slots, slots), 0)
    lane = lax.broadcasted_iota(jnp.int32, (slots, slots), 1)

    def as_column(row):
        return jnp.sum(
            jnp.where(sub == lane, row.astype(jnp.float32), 0.0), axis=1, keepdims=True
        ).astype(jnp.int32)

    drow, arow = dpos[...], apos[...]
    dcol, acol = as_column(drow), as_column(arow)

    def same(col, row):
        return (col >> 9) == (row >> 9)

    def ones(mask, axis):
        return jnp.sum(jnp.where(mask, 1.0, 0.0), axis=axis, keepdims=True).astype(jnp.int32)

    drank_row = ones(same(dcol, drow) & (sub < lane), 0)
    arank_row = ones(same(acol, arow) & (sub < lane), 0) + ones(same(dcol, arow), 0)
    drank_col = ones(same(dcol, drow) & (lane < sub), 1)
    arank_col = ones(same(acol, arow) & (lane < sub), 1) + ones(same(acol, drow), 1)
    dcode = (dcol >> 9) * CAP + drank_col
    acode = (acol >> 9) * CAP + arank_col
    asks[me, 0:1, :] = (((drow >> 9) * CAP + drank_row) << 9) + (drow & (rows - 1))
    asks[me, 1:2, :] = (((arow >> 9) * CAP + arank_row) << 9) + (arow & (rows - 1))
    spot = lax.broadcasted_iota(jnp.int32, (slots, n * CAP), 1)
    slot = lax.broadcasted_iota(jnp.int32, (slots, n * CAP), 0)
    live = slot < count[0]
    dhot[...] = jnp.where((spot == dcode) & live, 1.0, 0.0).astype(jnp.bfloat16)
    ahot[...] = jnp.where(spot == acode, 1.0, 0.0).astype(jnp.bfloat16)

    def widen(at, count):
        for c in range(lanes):
            padded[c, at + 8 : at + 8 + count, :] = feat[
                at : at + count, c * LANES : (c + 1) * LANES
            ].astype(jnp.float32)

    def conv_norm(at, count):
        total = jnp.zeros((count, LANES), jnp.float32)
        parts = []
        for c in range(lanes):
            cols = slice(c * LANES, (c + 1) * LANES)
            conv = taps[0:1, cols] * padded[c, at + 6 : at + 6 + count, :]
            for k in range(1, 5):
                conv = conv + taps[k : k + 1, cols] * padded[c, at + 6 + k : at + 6 + k + count, :]
            total = total + conv * conv
            parts.append(conv)
        mean = jnp.sum(total, axis=1, keepdims=True) * (1.0 / channels)
        scale = lax.rsqrt(mean + 1e-6)
        for c in range(lanes):
            cols = slice(c * LANES, (c + 1) * LANES)
            normed[at : at + count, cols] = (parts[c] * scale * gain[c : c + 1, :]).astype(
                jnp.bfloat16
            )

    loads[2].wait()
    loads[3].wait()
    widen(0, 16)
    widen(rows - 16, 16)
    for c in range(lanes):
        edge_out[0, 2 * c : 2 * c + 2, :] = padded[c, 8:10, :]
        edge_out[1, 2 * c : 2 * c + 2, :] = padded[c, rows + 6 : rows + 8, :]

    loads[4].wait()
    loads[5].wait()
    loads[6].wait()
    widen(16, 32)
    for at in range(16, 240, 32):
        if at + 32 < rows - 16:
            widen(at + 32, min(32, rows - 16 - at - 32))
        conv_norm(at, min(32, rows - 16 - at))

    pl.semaphore_wait(barrier, n - 1)

    def edge(i, step):
        return pltpu.make_async_remote_copy(
            edge_out.at[i],
            edge_in.at[i],
            edge_send.at[i],
            edge_recv.at[i],
            device_id={"seq": lax.rem(me + step, n)},
        )

    def ask(d):
        return pltpu.make_async_remote_copy(
            asks.at[me], asks.at[me], ask_send.at[d], ask_recv.at[d], device_id={"seq": ahead(d)}
        )

    before, after = edge(1, 1), edge(0, n - 1)
    before.start()
    after.start()

    @pl.loop(1, n)
    def _(d):
        ask(d).start()

    for at in range(240, rows - 16, 32):
        if at + 32 < rows - 16:
            widen(at + 32, min(32, rows - 16 - at - 32))
        conv_norm(at, min(32, rows - 16 - at))

    def encode(spans):
        for c in range(channels // WIDE):
            cols = slice(c * WIDE, (c + 1) * WIDE)
            source = jnp.concatenate([normed[a:b, :] for a, b in spans], axis=0)
            mixed = jnp.dot(source, point[:, cols], preferred_element_type=jnp.float32)
            at = 0
            for a, b in spans:
                part = mixed[at : at + b - a]
                at += b - a
                enc[a:b, cols] = (feat[a:b, cols].astype(jnp.float32) + gelu(part)).astype(
                    jnp.bfloat16
                )

    loads[7].wait()
    half = rows // 2
    encode([(16, 16 + half)])
    loads[8].wait()
    loads[9].wait()
    before.wait()
    after.wait()

    for c in range(lanes):
        padded[c, 6:8, :] = jnp.where(me == 0, 0.0, edge_in[1, 2 * c : 2 * c + 2, :])
        padded[c, rows + 8 : rows + 10, :] = jnp.where(
            me == n - 1, 0.0, edge_in[0, 2 * c : 2 * c + 2, :]
        )
    conv_norm(0, 16)
    conv_norm(rows - 16, 16)
    encode([(0, 16), (16 + half, rows)])

    @pl.loop(1, n)
    def _(d):
        ask(d).wait()


    target = me * CAP + lax.broadcasted_iota(jnp.int32, (CAP, slots), 0)
    place = lax.broadcasted_iota(jnp.int32, (CAP, rows), 1)
    for s in range(n):
        d, a = asks[s, 0:1, :], asks[s, 1:2, :]
        found = jnp.where((d >> 9) == target, (d & (rows - 1)).astype(jnp.float32), 0.0)
        found += jnp.where((a >> 9) == target, ((a & (rows - 1)) + rows).astype(jnp.float32), 0.0)
        index = jnp.sum(found, axis=1, keepdims=True).astype(jnp.int32)
        hot[s * CAP : (s + 1) * CAP, :] = jnp.where(
            (index & (rows - 1)) == place, 1.0, 0.0
        ).astype(jnp.bfloat16)
        kinds[s * CAP : (s + 1) * CAP, :] = jnp.broadcast_to(index, (CAP, LANES))

    for c in range(channels // WIDE):
        cols = slice(c * WIDE, (c + 1) * WIDE)
        picked[:, cols] = jnp.dot(
            hot[...], enc[:, cols], preferred_element_type=jnp.float32
        ).astype(jnp.bfloat16)

    def send(c, d):
        return pltpu.make_async_remote_copy(
            out_rows.at[c, ahead(d)],
            in_rows.at[c, me],
            row_send.at[c, d],
            row_recv.at[c, d],
            device_id={"seq": ahead(d)},
        )

    def hops(d):
        y, x = divmod(d, side)
        return min(y, side - y) + min(x, side - x)

    order = sorted(range(1, n), key=lambda d: -hops(d))
    is_accept = jnp.concatenate([kinds[...] >= rows] * (WIDE // LANES), axis=1)
    for c in range(width // WIDE):
        cols = slice(c * WIDE, (c + 1) * WIDE)
        left = jnp.dot(picked[...], donor[:, cols], preferred_element_type=jnp.float32)
        right = jnp.dot(picked[...], accept[:, cols], preferred_element_type=jnp.float32)
        out_rows[c] = jnp.where(is_accept, right, left).astype(jnp.bfloat16).reshape(n, CAP, WIDE)
        for d in order:
            send(c, d).start()

    for c in range(width // WIDE):
        in_rows[c, me] = out_rows[c, me]

        @pl.loop(1, n)
        def _(d):
            send(c, d).wait()


def finish(enc, in_rows, dhot, ahot, enc_hbm, junc_hbm, junc, sem):
    store = pltpu.make_async_copy(enc, enc_hbm, sem.at[0])
    store.start()
    blocks, n, cap, wide = in_rows.shape
    for c in range(blocks):
        got = in_rows[c].reshape(n * cap, wide)
        left = jnp.dot(dhot[...], got, preferred_element_type=jnp.float32)
        right = jnp.dot(ahot[...], got, preferred_element_type=jnp.float32)
        junc[:, c * wide : (c + 1) * wide] = (left / (1.0 + jnp.exp(-left)) * right).astype(
            jnp.bfloat16
        )
    last = pltpu.make_async_copy(junc, junc_hbm, sem.at[1])
    last.start()
    last.wait()
    store.wait()


def on_device(side, features, taps, gain, point, donor, accept, dpos, apos, counts):
    rows, channels = features.shape
    slots = dpos.shape[0]
    width = donor.shape[1]
    n = side * side
    blocks = width // WIDE
    f32, bf16, i32 = jnp.float32, jnp.bfloat16, jnp.int32
    dma = pltpu.SemaphoreType.DMA
    held = pl.pallas_call(
        functools.partial(kernel, side),
        out_shape=(
            pltpu.VMEM((rows, channels), bf16),
            pltpu.VMEM((blocks, n, CAP, WIDE), bf16),
            pltpu.VMEM((slots, n * CAP), bf16),
            pltpu.VMEM((slots, n * CAP), bf16),
        ),
        in_specs=[pl.BlockSpec(memory_space=pltpu.HBM)] * 8
        + [pl.BlockSpec(memory_space=pltpu.SMEM)],
        out_specs=[pl.BlockSpec(memory_space=pltpu.VMEM)] * 4,
        scratch_shapes=[
            pltpu.VMEM((rows, channels), bf16),
            pltpu.VMEM(taps.shape, f32),
            pltpu.VMEM((channels // LANES, LANES), f32),
            pltpu.VMEM((channels, channels), bf16),
            pltpu.VMEM((channels, width), bf16),
            pltpu.VMEM((channels, width), bf16),
            pltpu.VMEM((1, slots), i32),
            pltpu.VMEM((1, slots), i32),
            pltpu.VMEM((channels // LANES, rows + 16, LANES), f32),
            pltpu.VMEM((rows, channels), bf16),
            pltpu.VMEM((n * CAP, rows), bf16),
            pltpu.VMEM((n * CAP, LANES), i32),
            pltpu.VMEM((n * CAP, channels), bf16),
            pltpu.VMEM((2, 2 * channels // LANES, LANES), f32),
            pltpu.VMEM((2, 2 * channels // LANES, LANES), f32),
            pltpu.VMEM((n, 2, slots), i32),
            pltpu.VMEM((blocks, n, CAP, WIDE), bf16),
            dma((10,)),
            dma((2,)),
            dma((2,)),
            dma((n,)),
            dma((n,)),
            dma((blocks, n)),
            dma((blocks, n)),
        ],
        compiler_params=pltpu.CompilerParams(
            collective_id=0, has_side_effects=True, vmem_limit_bytes=40 * 1024 * 1024
        ),
    )(
        *(
            pltpu.with_memory_space_constraint(v, pltpu.HBM)
            for v in (
                features,
                taps,
                gain.reshape(channels // LANES, LANES),
                point,
                donor,
                accept,
                dpos.reshape(1, slots),
                apos.reshape(1, slots),
            )
        ),
        counts,
    )
    return pl.pallas_call(
        finish,
        out_shape=(
            jax.ShapeDtypeStruct((rows, channels), bf16),
            jax.ShapeDtypeStruct((slots, width), bf16),
        ),
        in_specs=[pl.BlockSpec(memory_space=pltpu.VMEM)] * 4,
        out_specs=[pl.BlockSpec(memory_space=pltpu.HBM)] * 2,
        scratch_shapes=[pltpu.VMEM((slots, width), bf16), dma((2,))],
        compiler_params=pltpu.CompilerParams(vmem_limit_bytes=8 * 1024 * 1024),
    )(*held)


def solution(mesh):
    side = 4
    placed = (
        P(("dp", "seq"), None),
        P(),
        P(),
        P(),
        P(),
        P(),
        P(("dp", "seq")),
        P(("dp", "seq")),
        P(("dp", "seq")),
    )
    return jax.shard_map(
        functools.partial(on_device, side),
        mesh=mesh,
        in_specs=placed,
        out_specs=(P(("dp", "seq"), None), P(("dp", "seq"), None)),
        check_vma=False,
    )
```

```python
import functools

import jax
import jax.numpy as jnp
from jax import lax
from jax.experimental import pallas as pl
from jax.experimental.pallas import tpu as pltpu
from jax.sharding import PartitionSpec as P

CAP = 16
LANES = 128
WIDE = 256


def gelu(v):
    return 0.5 * v * (1.0 + lax.erf(v * 0.7071067811865476))


def kernel(
    side,
    feat_hbm,
    taps_hbm,
    gain_hbm,
    point_hbm,
    donor_hbm,
    accept_hbm,
    dpos_hbm,
    apos_hbm,
    count,
    enc,
    in_rows,
    dhot,
    ahot,
    feat,
    taps,
    gain,
    point,
    donor,
    accept,
    dpos,
    apos,
    padded,
    normed,
    hot,
    kinds,
    picked,
    edge_out,
    edge_in,
    asks,
    out_rows,
    load_sem,
    edge_send,
    edge_recv,
    ask_send,
    ask_recv,
    row_send,
    row_recv,
):
    n = side * side
    rows, channels = feat.shape
    slots = dpos.shape[1]
    width = donor.shape[1]
    lanes = channels // LANES
    me = lax.axis_index("seq")
    my, mx = lax.div(me, side), lax.rem(me, side)

    ys = [lax.rem(my + d, side) * side for d in range(side)]
    xs = [lax.rem(mx + d, side) for d in range(side)]
    peers = [ys[d // side] + xs[d % side] for d in range(n)]

    def load(i, source, target):
        return pltpu.make_async_copy(source, target, load_sem.at[i])

    loads = [
        load(0, dpos_hbm, dpos),
        load(1, apos_hbm, apos),
        load(2, feat_hbm.at[0:16], feat.at[0:16]),
        load(3, feat_hbm.at[rows - 16 : rows], feat.at[rows - 16 : rows]),
        load(4, taps_hbm, taps),
        load(5, gain_hbm, gain),
        load(6, feat_hbm.at[16 : rows - 16], feat.at[16 : rows - 16]),
        load(7, point_hbm, point),
        load(8, donor_hbm, donor),
        load(9, accept_hbm, accept),
    ]
    barrier = pltpu.get_barrier_semaphore()

    for d in range(1, n):
        pl.semaphore_signal(barrier, inc=1, device_id={"seq": peers[d]})

    for one in loads:
        one.start()

    loads[0].wait()
    loads[1].wait()
    sub = lax.broadcasted_iota(jnp.int32, (slots, slots), 0)
    lane = lax.broadcasted_iota(jnp.int32, (slots, slots), 1)

    def as_column(row):
        return jnp.sum(
            jnp.where(sub == lane, row.astype(jnp.float32), 0.0), axis=1, keepdims=True
        ).astype(jnp.int32)

    drow, arow = dpos[...], apos[...]
    dcol, acol = as_column(drow), as_column(arow)

    def same(col, row):
        return (col >> 9) == (row >> 9)

    def ones(mask, axis):
        return jnp.sum(jnp.where(mask, 1.0, 0.0), axis=axis, keepdims=True).astype(jnp.int32)

    drank_row = ones(same(dcol, drow) & (sub < lane), 0)
    arank_row = ones(same(acol, arow) & (sub < lane), 0) + ones(same(dcol, arow), 0)
    drank_col = ones(same(dcol, drow) & (lane < sub), 1)
    arank_col = ones(same(acol, arow) & (lane < sub), 1) + ones(same(acol, drow), 1)
    dcode = (dcol >> 9) * CAP + drank_col
    acode = (acol >> 9) * CAP + arank_col
    asks[me, 0:1, :] = (((drow >> 9) * CAP + drank_row) << 9) + (drow & (rows - 1))
    asks[me, 1:2, :] = (((arow >> 9) * CAP + arank_row) << 9) + (arow & (rows - 1))
    spot = lax.broadcasted_iota(jnp.int32, (slots, n * CAP), 1)
    slot = lax.broadcasted_iota(jnp.int32, (slots, n * CAP), 0)
    live = slot < count[0]
    dhot[...] = jnp.where((spot == dcode) & live, 1.0, 0.0).astype(jnp.bfloat16)
    ahot[...] = jnp.where(spot == acode, 1.0, 0.0).astype(jnp.bfloat16)

    def widen(at, count):
        for c in range(lanes):
            padded[c, at + 8 : at + 8 + count, :] = feat[
                at : at + count, c * LANES : (c + 1) * LANES
            ].astype(jnp.float32)

    def conv_norm(at, count):
        total = jnp.zeros((count, LANES), jnp.float32)
        parts = []
        for c in range(lanes):
            cols = slice(c * LANES, (c + 1) * LANES)
            conv = taps[0:1, cols] * padded[c, at + 6 : at + 6 + count, :]
            for k in range(1, 5):
                conv = conv + taps[k : k + 1, cols] * padded[c, at + 6 + k : at + 6 + k + count, :]
            total = total + conv * conv
            parts.append(conv)
        mean = jnp.sum(total, axis=1, keepdims=True) * (1.0 / channels)
        scale = lax.rsqrt(mean + 1e-6)
        for c in range(lanes):
            cols = slice(c * LANES, (c + 1) * LANES)
            normed[at : at + count, cols] = (parts[c] * scale * gain[c : c + 1, :]).astype(
                jnp.bfloat16
            )

    loads[2].wait()
    loads[3].wait()
    widen(0, 16)
    widen(rows - 16, 16)
    for c in range(lanes):
        edge_out[0, 2 * c : 2 * c + 2, :] = padded[c, 8:10, :]
        edge_out[1, 2 * c : 2 * c + 2, :] = padded[c, rows + 6 : rows + 8, :]

    loads[4].wait()
    loads[5].wait()
    loads[6].wait()
    widen(16, 32)
    for at in range(16, 240, 32):
        if at + 32 < rows - 16:
            widen(at + 32, min(32, rows - 16 - at - 32))
        conv_norm(at, min(32, rows - 16 - at))

    pl.semaphore_wait(barrier, n - 1)

    def edge(i, step):
        return pltpu.make_async_remote_copy(
            edge_out.at[i],
            edge_in.at[i],
            edge_send.at[i],
            edge_recv.at[i],
            device_id={"seq": lax.rem(me + step, n)},
        )

    def ask(d):
        return pltpu.make_async_remote_copy(
            asks.at[me], asks.at[me], ask_send.at[d], ask_recv.at[d], device_id={"seq": peers[d]}
        )

    before, after = edge(1, 1), edge(0, n - 1)
    before.start()
    after.start()

    for d in range(1, n):
        ask(d).start()

    for at in range(240, rows - 16, 32):
        if at + 32 < rows - 16:
            widen(at + 32, min(32, rows - 16 - at - 32))
        conv_norm(at, min(32, rows - 16 - at))

    def encode(spans):
        for c in range(channels // WIDE):
            cols = slice(c * WIDE, (c + 1) * WIDE)
            source = jnp.concatenate([normed[a:b, :] for a, b in spans], axis=0)
            mixed = jnp.dot(source, point[:, cols], preferred_element_type=jnp.float32)
            at = 0
            for a, b in spans:
                part = mixed[at : at + b - a]
                at += b - a
                enc[a:b, cols] = (feat[a:b, cols].astype(jnp.float32) + gelu(part)).astype(
                    jnp.bfloat16
                )

    loads[7].wait()
    half = 384
    encode([(16, 16 + half)])
    loads[8].wait()
    loads[9].wait()
    before.wait()
    after.wait()

    for c in range(lanes):
        padded[c, 6:8, :] = jnp.where(me == 0, 0.0, edge_in[1, 2 * c : 2 * c + 2, :])
        padded[c, rows + 8 : rows + 10, :] = jnp.where(
            me == n - 1, 0.0, edge_in[0, 2 * c : 2 * c + 2, :]
        )
    conv_norm(0, 16)
    conv_norm(rows - 16, 16)
    encode([(0, 16), (16 + half, rows)])

    for d in range(1, n):
        ask(d).wait()


    target = me * CAP + lax.broadcasted_iota(jnp.int32, (CAP, slots), 0)
    place = lax.broadcasted_iota(jnp.int32, (CAP, rows), 1)
    for s in range(n):
        d, a = asks[s, 0:1, :], asks[s, 1:2, :]
        found = jnp.where((d >> 9) == target, (d & (rows - 1)).astype(jnp.float32), 0.0)
        found += jnp.where((a >> 9) == target, ((a & (rows - 1)) + rows).astype(jnp.float32), 0.0)
        index = jnp.sum(found, axis=1, keepdims=True).astype(jnp.int32)
        hot[s * CAP : (s + 1) * CAP, :] = jnp.where(
            (index & (rows - 1)) == place, 1.0, 0.0
        ).astype(jnp.bfloat16)
        kinds[s * CAP : (s + 1) * CAP, :] = jnp.broadcast_to(index, (CAP, LANES))

    for c in range(channels // WIDE):
        cols = slice(c * WIDE, (c + 1) * WIDE)
        picked[:, cols] = jnp.dot(
            hot[...], enc[:, cols], preferred_element_type=jnp.float32
        ).astype(jnp.bfloat16)

    def send(c, d):
        return pltpu.make_async_remote_copy(
            out_rows.at[c, peers[d]],
            in_rows.at[c, me],
            row_send.at[c, d],
            row_recv.at[c, d],
            device_id={"seq": peers[d]},
        )

    def hops(d):
        y, x = divmod(d, side)
        return min(y, side - y) + min(x, side - x)

    order = sorted(range(1, n), key=lambda d: -hops(d))
    is_accept = jnp.concatenate([kinds[...] >= rows] * (WIDE // LANES), axis=1)
    for c in range(width // WIDE):
        cols = slice(c * WIDE, (c + 1) * WIDE)
        left = jnp.dot(picked[...], donor[:, cols], preferred_element_type=jnp.float32)
        right = jnp.dot(picked[...], accept[:, cols], preferred_element_type=jnp.float32)
        out_rows[c] = jnp.where(is_accept, right, left).astype(jnp.bfloat16).reshape(n, CAP, WIDE)
        for d in order:
            send(c, d).start()

    for c in range(width // WIDE):
        in_rows[c, me] = out_rows[c, me]
        for d in order:
            send(c, d).wait()


def finish(enc, in_rows, dhot, ahot, enc_hbm, junc_hbm, junc, sem):
    store = pltpu.make_async_copy(enc, enc_hbm, sem.at[0])
    store.start()
    blocks, n, cap, wide = in_rows.shape
    for c in range(blocks):
        got = in_rows[c].reshape(n * cap, wide)
        left = jnp.dot(dhot[...], got, preferred_element_type=jnp.float32)
        right = jnp.dot(ahot[...], got, preferred_element_type=jnp.float32)
        junc[:, c * wide : (c + 1) * wide] = (left / (1.0 + jnp.exp(-left)) * right).astype(
            jnp.bfloat16
        )
    last = pltpu.make_async_copy(junc, junc_hbm, sem.at[1])
    last.start()
    last.wait()
    store.wait()


def on_device(side, features, taps, gain, point, donor, accept, dpos, apos, counts):
    rows, channels = features.shape
    slots = dpos.shape[0]
    width = donor.shape[1]
    n = side * side
    blocks = width // WIDE
    f32, bf16, i32 = jnp.float32, jnp.bfloat16, jnp.int32
    dma = pltpu.SemaphoreType.DMA
    held = pl.pallas_call(
        functools.partial(kernel, side),
        out_shape=(
            pltpu.VMEM((rows, channels), bf16),
            pltpu.VMEM((blocks, n, CAP, WIDE), bf16),
            pltpu.VMEM((slots, n * CAP), bf16),
            pltpu.VMEM((slots, n * CAP), bf16),
        ),
        in_specs=[pl.BlockSpec(memory_space=pltpu.HBM)] * 8
        + [pl.BlockSpec(memory_space=pltpu.SMEM)],
        out_specs=[pl.BlockSpec(memory_space=pltpu.VMEM)] * 4,
        scratch_shapes=[
            pltpu.VMEM((rows, channels), bf16),
            pltpu.VMEM(taps.shape, f32),
            pltpu.VMEM((channels // LANES, LANES), f32),
            pltpu.VMEM((channels, channels), bf16),
            pltpu.VMEM((channels, width), bf16),
            pltpu.VMEM((channels, width), bf16),
            pltpu.VMEM((1, slots), i32),
            pltpu.VMEM((1, slots), i32),
            pltpu.VMEM((channels // LANES, rows + 16, LANES), f32),
            pltpu.VMEM((rows, channels), bf16),
            pltpu.VMEM((n * CAP, rows), bf16),
            pltpu.VMEM((n * CAP, LANES), i32),
            pltpu.VMEM((n * CAP, channels), bf16),
            pltpu.VMEM((2, 2 * channels // LANES, LANES), f32),
            pltpu.VMEM((2, 2 * channels // LANES, LANES), f32),
            pltpu.VMEM((n, 2, slots), i32),
            pltpu.VMEM((blocks, n, CAP, WIDE), bf16),
            dma((10,)),
            dma((2,)),
            dma((2,)),
            dma((n,)),
            dma((n,)),
            dma((blocks, n)),
            dma((blocks, n)),
        ],
        compiler_params=pltpu.CompilerParams(
            collective_id=0, has_side_effects=True, vmem_limit_bytes=40 * 1024 * 1024
        ),
    )(
        *(
            pltpu.with_memory_space_constraint(v, pltpu.HBM)
            for v in (
                features,
                taps,
                gain.reshape(channels // LANES, LANES),
                point,
                donor,
                accept,
                dpos.reshape(1, slots),
                apos.reshape(1, slots),
            )
        ),
        counts,
    )
    return pl.pallas_call(
        finish,
        out_shape=(
            jax.ShapeDtypeStruct((rows, channels), bf16),
            jax.ShapeDtypeStruct((slots, width), bf16),
        ),
        in_specs=[pl.BlockSpec(memory_space=pltpu.VMEM)] * 4,
        out_specs=[pl.BlockSpec(memory_space=pltpu.HBM)] * 2,
        scratch_shapes=[pltpu.VMEM((slots, width), bf16), dma((2,))],
        compiler_params=pltpu.CompilerParams(vmem_limit_bytes=8 * 1024 * 1024),
    )(*held)


def solution(mesh):
    side = 4
    placed = (
        P(("dp", "seq"), None),
        P(),
        P(),
        P(),
        P(),
        P(),
        P(("dp", "seq")),
        P(("dp", "seq")),
        P(("dp", "seq")),
    )
    return jax.shard_map(
        functools.partial(on_device, side),
        mesh=mesh,
        in_specs=placed,
        out_specs=(P(("dp", "seq"), None), P(("dp", "seq"), None)),
        check_vma=False,
    )
```

```python
import functools

import jax
import jax.numpy as jnp
from jax import lax
from jax.experimental import pallas as pl
from jax.experimental.pallas import tpu as pltpu
from jax.sharding import PartitionSpec as P

CAP = 16
LANES = 128
WIDE = 256


def gelu(v):
    return 0.5 * v * (1.0 + lax.erf(v * 0.7071067811865476))


def kernel(
    side,
    feat_hbm,
    taps_hbm,
    gain_hbm,
    point_hbm,
    donor_hbm,
    accept_hbm,
    dpos_hbm,
    apos_hbm,
    count,
    enc,
    in_rows,
    dhot,
    ahot,
    feat,
    taps,
    gain,
    point,
    donor,
    accept,
    dpos,
    apos,
    padded,
    normed,
    hot,
    kinds,
    picked,
    edge_out,
    edge_in,
    asks,
    out_rows,
    load_sem,
    edge_send,
    edge_recv,
    ask_send,
    ask_recv,
    row_send,
    row_recv,
):
    n = side * side
    rows, channels = feat.shape
    slots = dpos.shape[1]
    width = donor.shape[1]
    lanes = channels // LANES
    me = lax.axis_index("seq")
    my, mx = lax.div(me, side), lax.rem(me, side)

    ys = [lax.rem(my + d, side) * side for d in range(side)]
    xs = [lax.rem(mx + d, side) for d in range(side)]
    peers = [ys[d // side] + xs[d % side] for d in range(n)]

    def load(i, source, target):
        return pltpu.make_async_copy(source, target, load_sem.at[i])

    loads = [
        load(0, dpos_hbm, dpos),
        load(1, apos_hbm, apos),
        load(2, feat_hbm.at[0:16], feat.at[0:16]),
        load(3, feat_hbm.at[rows - 16 : rows], feat.at[rows - 16 : rows]),
        load(4, taps_hbm, taps),
        load(5, gain_hbm, gain),
        load(6, feat_hbm.at[16 : rows - 16], feat.at[16 : rows - 16]),
        load(7, point_hbm, point),
        load(8, donor_hbm, donor),
        load(9, accept_hbm, accept),
    ]
    barrier = pltpu.get_barrier_semaphore()

    for d in range(1, n):
        pl.semaphore_signal(barrier, inc=1, device_id={"seq": peers[d]})

    for one in loads:
        one.start()

    loads[0].wait()
    loads[1].wait()
    sub = lax.broadcasted_iota(jnp.int32, (slots, slots), 0)
    lane = lax.broadcasted_iota(jnp.int32, (slots, slots), 1)

    def as_column(row):
        return jnp.sum(
            jnp.where(sub == lane, row.astype(jnp.float32), 0.0), axis=1, keepdims=True
        ).astype(jnp.int32)

    drow, arow = dpos[...], apos[...]
    dcol, acol = as_column(drow), as_column(arow)

    def same(col, row):
        return (col >> 9) == (row >> 9)

    def ones(mask, axis):
        return jnp.sum(jnp.where(mask, 1.0, 0.0), axis=axis, keepdims=True).astype(jnp.int32)

    drank_row = ones(same(dcol, drow) & (sub < lane), 0)
    arank_row = ones(same(acol, arow) & (sub < lane), 0) + ones(same(dcol, arow), 0)
    drank_col = ones(same(dcol, drow) & (lane < sub), 1)
    arank_col = ones(same(acol, arow) & (lane < sub), 1) + ones(same(acol, drow), 1)
    dcode = (dcol >> 9) * CAP + drank_col
    acode = (acol >> 9) * CAP + arank_col
    asks[me, 0:1, :] = (((drow >> 9) * CAP + drank_row) << 9) + (drow & (rows - 1))
    asks[me, 1:2, :] = (((arow >> 9) * CAP + arank_row) << 9) + (arow & (rows - 1))
    spot = lax.broadcasted_iota(jnp.int32, (slots, n * CAP), 1)
    slot = lax.broadcasted_iota(jnp.int32, (slots, n * CAP), 0)
    live = slot < count[0]
    dhot[...] = jnp.where((spot == dcode) & live, 1.0, 0.0).astype(jnp.bfloat16)
    ahot[...] = jnp.where(spot == acode, 1.0, 0.0).astype(jnp.bfloat16)

    def widen(at, count):
        for c in range(lanes):
            padded[c, at + 8 : at + 8 + count, :] = feat[
                at : at + count, c * LANES : (c + 1) * LANES
            ].astype(jnp.float32)

    def conv_norm(at, count):
        total = jnp.zeros((count, LANES), jnp.float32)
        parts = []
        for c in range(lanes):
            cols = slice(c * LANES, (c + 1) * LANES)
            conv = taps[0:1, cols] * padded[c, at + 6 : at + 6 + count, :]
            for k in range(1, 5):
                conv = conv + taps[k : k + 1, cols] * padded[c, at + 6 + k : at + 6 + k + count, :]
            total = total + conv * conv
            parts.append(conv)
        mean = jnp.sum(total, axis=1, keepdims=True) * (1.0 / channels)
        scale = lax.rsqrt(mean + 1e-6)
        for c in range(lanes):
            cols = slice(c * LANES, (c + 1) * LANES)
            normed[at : at + count, cols] = (parts[c] * scale * gain[c : c + 1, :]).astype(
                jnp.bfloat16
            )

    loads[2].wait()
    loads[3].wait()
    widen(0, 16)
    widen(rows - 16, 16)
    for c in range(lanes):
        edge_out[0, 2 * c : 2 * c + 2, :] = padded[c, 8:10, :]
        edge_out[1, 2 * c : 2 * c + 2, :] = padded[c, rows + 6 : rows + 8, :]

    loads[4].wait()
    loads[5].wait()
    loads[6].wait()
    widen(16, 32)
    for at in range(16, 240, 32):
        if at + 32 < rows - 16:
            widen(at + 32, min(32, rows - 16 - at - 32))
        conv_norm(at, min(32, rows - 16 - at))

    pl.semaphore_wait(barrier, n - 1)

    def edge(i, step):
        return pltpu.make_async_remote_copy(
            edge_out.at[i],
            edge_in.at[i],
            edge_send.at[i],
            edge_recv.at[i],
            device_id={"seq": lax.rem(me + step, n)},
        )

    def ask(d):
        return pltpu.make_async_remote_copy(
            asks.at[me], asks.at[me], ask_send.at[d], ask_recv.at[d], device_id={"seq": peers[d]}
        )

    before, after = edge(1, 1), edge(0, n - 1)
    before.start()
    after.start()

    for d in range(1, n):
        ask(d).start()

    for at in range(240, rows - 16, 32):
        if at + 32 < rows - 16:
            widen(at + 32, min(32, rows - 16 - at - 32))
        conv_norm(at, min(32, rows - 16 - at))

    def encode(spans):
        for c in range(channels // WIDE):
            cols = slice(c * WIDE, (c + 1) * WIDE)
            source = jnp.concatenate([normed[a:b, :] for a, b in spans], axis=0)
            mixed = jnp.dot(source, point[:, cols], preferred_element_type=jnp.float32)
            at = 0
            for a, b in spans:
                part = mixed[at : at + b - a]
                at += b - a
                enc[a:b, cols] = (feat[a:b, cols].astype(jnp.float32) + gelu(part)).astype(
                    jnp.bfloat16
                )

    loads[7].wait()
    half = 384
    encode([(16, 16 + half)])
    loads[8].wait()
    loads[9].wait()
    before.wait()
    after.wait()

    for c in range(lanes):
        padded[c, 6:8, :] = jnp.where(me == 0, 0.0, edge_in[1, 2 * c : 2 * c + 2, :])
        padded[c, rows + 8 : rows + 10, :] = jnp.where(
            me == n - 1, 0.0, edge_in[0, 2 * c : 2 * c + 2, :]
        )
    conv_norm(0, 16)
    conv_norm(rows - 16, 16)
    encode([(0, 16), (16 + half, rows)])

    for d in range(1, n):
        ask(d).wait()


    def hops(d):
        y, x = divmod(d, side)
        return min(y, side - y) + min(x, side - x)

    order = sorted(range(n), key=lambda d: -hops(d))
    target = me * CAP + lax.broadcasted_iota(jnp.int32, (CAP, slots), 0)
    place = lax.broadcasted_iota(jnp.int32, (CAP, rows), 1)

    def send(c, i):
        d = order[i]
        return pltpu.make_async_remote_copy(
            out_rows.at[c, i],
            in_rows.at[c, me],
            row_send.at[c, d],
            row_recv.at[c, d],
            device_id={"seq": peers[d]},
        )

    group = n // 2
    for g in range(0, n, group):
        span = slice(g * CAP, (g + group) * CAP)
        for i in range(g, g + group):
            d, a = asks[peers[order[i]], 0:1, :], asks[peers[order[i]], 1:2, :]
            found = jnp.where((d >> 9) == target, (d & (rows - 1)).astype(jnp.float32), 0.0)
            found += jnp.where(
                (a >> 9) == target, ((a & (rows - 1)) + rows).astype(jnp.float32), 0.0
            )
            index = jnp.sum(found, axis=1, keepdims=True).astype(jnp.int32)
            hot[i * CAP : (i + 1) * CAP, :] = jnp.where(
                (index & (rows - 1)) == place, 1.0, 0.0
            ).astype(jnp.bfloat16)
            kinds[i * CAP : (i + 1) * CAP, :] = jnp.broadcast_to(index, (CAP, LANES))
        for c in range(channels // WIDE):
            cols = slice(c * WIDE, (c + 1) * WIDE)
            picked[span, cols] = jnp.dot(
                hot[span, :], enc[:, cols], preferred_element_type=jnp.float32
            ).astype(jnp.bfloat16)
        is_accept = jnp.concatenate([kinds[span, :] >= rows] * (WIDE // LANES), axis=1)
        for c in range(width // WIDE):
            cols = slice(c * WIDE, (c + 1) * WIDE)
            left = jnp.dot(picked[span, :], donor[:, cols], preferred_element_type=jnp.float32)
            right = jnp.dot(picked[span, :], accept[:, cols], preferred_element_type=jnp.float32)
            out_rows[c, g : g + group] = (
                jnp.where(is_accept, right, left).astype(jnp.bfloat16).reshape(group, CAP, WIDE)
            )
            for i in range(g, min(g + group, n - 1)):
                send(c, i).start()

    for c in range(width // WIDE):
        in_rows[c, me] = out_rows[c, n - 1]
    for g in range(0, n, group):
        for c in range(width // WIDE):
            for i in range(g, min(g + group, n - 1)):
                send(c, i).wait()


def finish(enc, in_rows, dhot, ahot, enc_hbm, junc_hbm, junc, sem):
    store = pltpu.make_async_copy(enc, enc_hbm, sem.at[0])
    store.start()
    blocks, n, cap, wide = in_rows.shape
    for c in range(blocks):
        got = in_rows[c].reshape(n * cap, wide)
        left = jnp.dot(dhot[...], got, preferred_element_type=jnp.float32)
        right = jnp.dot(ahot[...], got, preferred_element_type=jnp.float32)
        junc[:, c * wide : (c + 1) * wide] = (left / (1.0 + jnp.exp(-left)) * right).astype(
            jnp.bfloat16
        )
    last = pltpu.make_async_copy(junc, junc_hbm, sem.at[1])
    last.start()
    last.wait()
    store.wait()


def on_device(side, features, taps, gain, point, donor, accept, dpos, apos, counts):
    rows, channels = features.shape
    slots = dpos.shape[0]
    width = donor.shape[1]
    n = side * side
    blocks = width // WIDE
    f32, bf16, i32 = jnp.float32, jnp.bfloat16, jnp.int32
    dma = pltpu.SemaphoreType.DMA
    held = pl.pallas_call(
        functools.partial(kernel, side),
        out_shape=(
            pltpu.VMEM((rows, channels), bf16),
            pltpu.VMEM((blocks, n, CAP, WIDE), bf16),
            pltpu.VMEM((slots, n * CAP), bf16),
            pltpu.VMEM((slots, n * CAP), bf16),
        ),
        in_specs=[pl.BlockSpec(memory_space=pltpu.HBM)] * 8
        + [pl.BlockSpec(memory_space=pltpu.SMEM)],
        out_specs=[pl.BlockSpec(memory_space=pltpu.VMEM)] * 4,
        scratch_shapes=[
            pltpu.VMEM((rows, channels), bf16),
            pltpu.VMEM(taps.shape, f32),
            pltpu.VMEM((channels // LANES, LANES), f32),
            pltpu.VMEM((channels, channels), bf16),
            pltpu.VMEM((channels, width), bf16),
            pltpu.VMEM((channels, width), bf16),
            pltpu.VMEM((1, slots), i32),
            pltpu.VMEM((1, slots), i32),
            pltpu.VMEM((channels // LANES, rows + 16, LANES), f32),
            pltpu.VMEM((rows, channels), bf16),
            pltpu.VMEM((n * CAP, rows), bf16),
            pltpu.VMEM((n * CAP, LANES), i32),
            pltpu.VMEM((n * CAP, channels), bf16),
            pltpu.VMEM((2, 2 * channels // LANES, LANES), f32),
            pltpu.VMEM((2, 2 * channels // LANES, LANES), f32),
            pltpu.VMEM((n, 2, slots), i32),
            pltpu.VMEM((blocks, n, CAP, WIDE), bf16),
            dma((10,)),
            dma((2,)),
            dma((2,)),
            dma((n,)),
            dma((n,)),
            dma((blocks, n)),
            dma((blocks, n)),
        ],
        compiler_params=pltpu.CompilerParams(
            collective_id=0, has_side_effects=True, vmem_limit_bytes=40 * 1024 * 1024
        ),
    )(
        *(
            pltpu.with_memory_space_constraint(v, pltpu.HBM)
            for v in (
                features,
                taps,
                gain.reshape(channels // LANES, LANES),
                point,
                donor,
                accept,
                dpos.reshape(1, slots),
                apos.reshape(1, slots),
            )
        ),
        counts,
    )
    return pl.pallas_call(
        finish,
        out_shape=(
            jax.ShapeDtypeStruct((rows, channels), bf16),
            jax.ShapeDtypeStruct((slots, width), bf16),
        ),
        in_specs=[pl.BlockSpec(memory_space=pltpu.VMEM)] * 4,
        out_specs=[pl.BlockSpec(memory_space=pltpu.HBM)] * 2,
        scratch_shapes=[pltpu.VMEM((slots, width), bf16), dma((2,))],
        compiler_params=pltpu.CompilerParams(vmem_limit_bytes=8 * 1024 * 1024),
    )(*held)


def solution(mesh):
    side = 4
    placed = (
        P(("dp", "seq"), None),
        P(),
        P(),
        P(),
        P(),
        P(),
        P(("dp", "seq")),
        P(("dp", "seq")),
        P(("dp", "seq")),
    )
    return jax.shard_map(
        functools.partial(on_device, side),
        mesh=mesh,
        in_specs=placed,
        out_specs=(P(("dp", "seq"), None), P(("dp", "seq"), None)),
        check_vma=False,
    )
```
